32 devices in a mesh: grp: 2 (over y), tgt: 8 (over z, x), src: 2 (over core).
Axes of the slice: x: 2, y: 2, z: 4, core: 2. Of those that a mesh axis runs over, the one named last changes fastest.
Arguments:
- sources: bfloat16 [131072, 32], P(('grp', 'tgt', 'src')), parts along dimension 0, may hold values from -6 to 6
- leaf_order: int32 [131072], P(('grp', 'tgt', 'src')), parts along dimension 0, may hold values from 0 to 4095, as said below
- skeleton: int32 [2048, 32], P(('grp', 'tgt')), parts along dimension 0, may hold values from 0 to 63, as said below
- interp_rows: bfloat16 [2, 2048, 32, 64], P(None, ('grp', 'tgt')), parts along dimension 1, may hold values from -0.75 to 0.75
- near_tiles: bfloat16 [2, 2048, 64, 64], P(None, ('grp', 'tgt'), 'src'), parts along dimension 1, may hold values from -0.75 to 0.75
- target_basis: bfloat16 [2, 2048, 64, 32], P(None, ('grp', 'tgt'), 'src'), parts along dimension 1, may hold values from -0.75 to 0.75
- level_maps: float32 [2, 20, 2, 32, 64], P(None, 'grp'), parts along dimension 1, may hold values from -0.5 to 0.5
Outputs:
- potential: bfloat16 [2, 131072, 32], P(None, ('grp', 'tgt', 'src')), parts along dimension 1
The draws below stay inside these ranges and needn't reach their ends.
There are 2 independent parts, one for each index of `grp`. The reference program is written for one: setup_inputs(seed, part) draws one part's arguments, and reference() takes and returns one part's arrays. A program takes and returns all parts, laid end to end along the dimension named above; each array names one. Nothing has to cross between parts.
Inputs may be any that keep to these rules, and one draw needn't show every extreme that they name: `leaf_order`: each aligned block of 4096 entries is a permutation of the positions 0 .. 4095 within that block. `skeleton`: each row holds 32 distinct points of its leaf.
All inputs are finite; a program needn't handle non-finite values.
Results may differ from the reference program's by a relative error of at most 0.0045.
Values may be sent and summed in bfloat16 or wider, within the bound.
A program may use at most 64 MiB of HBM per device.

```python
import jax
import jax.numpy as jnp
from jax import lax

R = 32
NRHS = 32
LEAF = 64
B_DEV = 128
LEVELS = 10
NBOX = 1024
LEAFH = 32
NPTS = 65536
N_TGT = 8
N_SRC = 2


def draw_leaf_order(key, part):
    key = jax.random.fold_in(key, 11)
    block_total = N_TGT * N_SRC
    point_count = B_DEV * LEAF // N_SRC
    block_keys = jax.random.split(key, block_total)
    orders = jax.vmap(lambda block_key: jax.random.permutation(block_key, point_count))(block_keys)
    return orders.astype(jnp.int32).reshape(-1)


def draw_skeleton(key, part):
    key = jax.random.fold_in(key, 23)
    box_keys = jax.random.split(key, NBOX)
    chosen = jax.vmap(lambda box_key: jax.random.permutation(box_key, LEAF)[:R])(box_keys)
    return chosen.astype(jnp.int32)


def block_scale(own_key, extent, shards, low, largest):
    gain, own = 1.0, jax.random.fold_in(own_key, 6)
    for position, parts in shards:
        heights = jnp.exp(jax.random.uniform(jax.random.fold_in(own, position), (parts,), jnp.float32, low / len(shards), largest / len(shards)))
        gain = gain * jnp.repeat(heights, extent[position] // parts).reshape([-1 if axis == position else 1 for axis in range(len(extent))])
    return gain


def centred(rng, dims, width, limit, cuts=(), kind=jnp.bfloat16):
    level = block_scale(rng, dims, cuts, -0.22, 0.18) if cuts else 1.0
    result = jax.random.normal(rng, dims, jnp.float32) * width * level
    return jnp.minimum(jnp.maximum(result, -limit), limit).astype(kind)


def setup_inputs(seed: int = 0, part: int = 0) -> dict:
    key_of = jax.random.split(jax.random.key(seed), 8)
    part_keys = jax.random.split(jax.random.fold_in(key_of[7], part), 8)
    return {
        "sources": centred(part_keys[0], (NPTS, NRHS), 1.0, 6.0, ((0, 16),)),
        "leaf_order": draw_leaf_order(jax.random.fold_in(jax.random.fold_in(key_of[7], part), 71), part),
        "skeleton": draw_skeleton(jax.random.fold_in(jax.random.fold_in(key_of[7], part), 71), part),
        "interp_rows": centred(part_keys[3], (2, NBOX, R, LEAF), LEAF ** -0.5, 0.75, ((1, 8),)),
        "near_tiles": centred(part_keys[4], (2, NBOX, LEAF, LEAF), LEAF ** -0.5, 0.75, ((1, 8), (2, 2))),
        "target_basis": centred(part_keys[5], (2, NBOX, LEAF, R), (2 * R) ** -0.5, 0.75, ((1, 8), (2, 2))),
        "level_maps": centred(part_keys[6], (2, LEVELS, 2, R, 2 * R), (4 * R) ** -0.5, 0.5, (), jnp.float32),
    }


def complex_mix(real_map, imag_map, joined):
    real_part = joined[..., 0, :, :]
    imag_part = joined[..., 1, :, :]
    out_real = jnp.einsum('rq,...qh->...rh', real_map, real_part, precision=lax.Precision.HIGHEST) - jnp.einsum('rq,...qh->...rh', imag_map, imag_part, precision=lax.Precision.HIGHEST)
    out_imag = jnp.einsum('rq,...qh->...rh', real_map, imag_part, precision=lax.Precision.HIGHEST) + jnp.einsum('rq,...qh->...rh', imag_map, real_part, precision=lax.Precision.HIGHEST)
    return jnp.stack([out_real, out_imag], axis=-3)


def apply_level(coefficients, matrices, level_bit):
    row_count = coefficients.shape[0]
    distance = 2 ** level_bit
    trailing = coefficients.shape[1:]
    grouped = coefficients.reshape((row_count // (2 * distance), 2, distance) + trailing)
    joined = jnp.concatenate([grouped[:, 0], grouped[:, 1]], axis=-2)
    lower_half = complex_mix(matrices[0, 0], matrices[1, 0], joined)
    upper_half = complex_mix(matrices[0, 1], matrices[1, 1], joined)
    return jnp.stack([lower_half, upper_half], axis=1).reshape(coefficients.shape)


def reference(sources, leaf_order, skeleton, interp_rows, near_tiles, target_basis, level_maps):
    block_rows = B_DEV * LEAFH
    block_start = (jnp.arange(NPTS, dtype=jnp.int32) // block_rows) * block_rows
    global_order = leaf_order.astype(jnp.int32) + block_start
    permuted = jnp.take(sources, global_order, axis=0)
    leaves = permuted.reshape(N_TGT, N_SRC, B_DEV, LEAFH, NRHS).transpose(0, 2, 1, 3, 4).reshape(NBOX, LEAF, NRHS)
    leaves_wide = leaves.astype(jnp.float32)
    indices = jnp.broadcast_to(skeleton.astype(jnp.int32)[:, :, None], (NBOX, R, NRHS))
    picked = jnp.take_along_axis(leaves_wide, indices, axis=1)
    interp_wide = interp_rows.astype(jnp.float32)
    coeff_real = picked + jnp.einsum('brj,bjh->brh', interp_wide[0], leaves_wide, precision=lax.Precision.HIGHEST)
    coeff_imag = jnp.einsum('brj,bjh->brh', interp_wide[1], leaves_wide, precision=lax.Precision.HIGHEST)
    coefficients = jnp.stack([coeff_real, coeff_imag], axis=1)
    for level_index in range(LEVELS):
        coefficients = apply_level(coefficients, level_maps[:, level_index], level_index)
    rounded = coefficients.astype(jnp.bfloat16).astype(jnp.float32)
    basis_wide = target_basis.astype(jnp.float32)
    tiles_wide = near_tiles.astype(jnp.float32)
    far_real = jnp.einsum('bir,brh->bih', basis_wide[0], rounded[:, 0], precision=lax.Precision.HIGHEST) - jnp.einsum('bir,brh->bih', basis_wide[1], rounded[:, 1], precision=lax.Precision.HIGHEST)
    far_imag = jnp.einsum('bir,brh->bih', basis_wide[0], rounded[:, 1], precision=lax.Precision.HIGHEST) + jnp.einsum('bir,brh->bih', basis_wide[1], rounded[:, 0], precision=lax.Precision.HIGHEST)
    near_real = jnp.einsum('bij,bjh->bih', tiles_wide[0], leaves_wide, precision=lax.Precision.HIGHEST)
    near_imag = jnp.einsum('bij,bjh->bih', tiles_wide[1], leaves_wide, precision=lax.Precision.HIGHEST)
    field = jnp.stack([far_real + near_real, far_imag + near_imag], axis=0)
    potential = field.reshape(2, N_TGT, B_DEV, N_SRC, LEAFH, NRHS).transpose(0, 1, 3, 2, 4, 5).reshape(2, NPTS, NRHS)
    return potential.astype(jnp.bfloat16)
```

```python
import jax
import jax.numpy as jnp
from jax import lax
from jax.experimental import pallas as pl
from jax.experimental.pallas import tpu as pltpu
from jax.sharding import PartitionSpec as P

F32 = jnp.float32
BF16 = jnp.bfloat16
CHUNKS = 2
LOW = 256
VM = pl.BlockSpec(memory_space=pltpu.VMEM)
PARAMS = pltpu.CompilerParams(vmem_limit_bytes=40 * 2**20)


def from_partner(value, axis, distance):
    mask = 2**distance
    pairs = [(source, source ^ mask) for source in range(lax.axis_size(axis))]
    return lax.ppermute(value, axis, pairs)


def gather_kernel(src_ref, idx_ref, out_ref, table):
    rhs, points = src_ref.shape
    high_count = points // LOW
    boxes = out_ref.shape[2]
    per = LOW // boxes
    for high in range(high_count):
        table[pl.ds(high * rhs, rhs), :] = src_ref[:, pl.ds(high * LOW, LOW)]

    def step(g, carry):
        index = idx_ref[pl.ds(g, 1), :]
        low = index % LOW
        high_of = jnp.broadcast_to(index // LOW, (rhs, LOW))
        rows = lax.broadcasted_iota(jnp.int32, (LOW, LOW), 0)
        onehot = jnp.where(rows == low, 1.0, 0.0).astype(BF16)
        found = jnp.dot(table[...], onehot, preferred_element_type=F32)
        total = jnp.zeros((rhs, LOW), F32)
        for high in range(high_count):
            total = jnp.where(high_of == high, found[high * rhs:(high + 1) * rhs], total)
        for part in range(per):
            out_ref[g * per + part] = total[:, part * boxes:(part + 1) * boxes].astype(BF16)
        return carry

    lax.fori_loop(0, idx_ref.shape[0], step, 0)


def split(value):
    high = value.astype(BF16)
    return high, (value - high.astype(F32)).astype(BF16)


def level_block(lm_ref, level, upper):
    real = lm_ref[0, level, upper]
    imag = lm_ref[1, level, upper]
    top = jnp.concatenate([real, -imag], axis=1)
    bottom = jnp.concatenate([imag, real], axis=1)
    return jnp.concatenate([top, bottom], axis=0)


def join(lower, higher):
    half = lower.shape[0] // 2
    return jnp.concatenate([lower[:half], higher[:half], lower[half:], higher[half:]], axis=0)


def dot(a, b):
    return jnp.dot(a, b, preferred_element_type=F32)


def dot3(a, b):
    a_high, a_low = split(a)
    b_high, b_low = split(b)
    return dot(a_high, b_high) + dot(a_high, b_low) + dot(a_low, b_high)


def local_kernel(local_levels, leaves_ref, skel_ref, interp_ref, lm_ref, *rest):
    outs = rest[: 2 * CHUNKS]
    wide, weights, coeff, vals = rest[2 * CHUNKS:]
    points, rhs, boxes = leaves_ref.shape
    rank = skel_ref.shape[0]
    width = rhs // lax.axis_size("src")
    start = pl.multiple_of(lax.axis_index("src") * width, width)
    wide[...] = leaves_ref[:, pl.ds(start, width), :].astype(F32)
    block = 4
    rows = lax.broadcasted_iota(jnp.int32, (points, boxes), 0)

    def ranks(g, carry):
        for k in range(block):
            r = g * block + k
            pick = jnp.where(rows == skel_ref[pl.ds(r, 1), :], 1.0, 0.0)
            weights[2 * k] = interp_ref[0, r].astype(F32) + pick
            weights[2 * k + 1] = interp_ref[1, r].astype(F32)
        acc = [jnp.zeros((width, boxes), F32) for _ in range(2 * block)]
        for j in range(points):
            leaf = wide[j]
            for k in range(2 * block):
                acc[k] = acc[k] + weights[k, pl.ds(j, 1), :] * leaf
        for k in range(block):
            for c in range(2):
                at = pl.multiple_of((c * rank + g * block + k) * width, width)
                coeff[pl.ds(at, width), :] = acc[2 * k + c]
        return carry

    lax.fori_loop(0, rank // block, ranks, 0)
    for h in range(width):
        vals[:, h * boxes:(h + 1) * boxes] = coeff[pl.ds(h, 2 * rank, stride=width), :]
    cols = width * boxes
    lane = lax.broadcasted_iota(jnp.int32, (2 * rank, boxes), 1)
    for level in range(local_levels):
        distance = 2**level
        bit = (lane // distance) % 2 == 1
        full = jnp.concatenate([level_block(lm_ref, level, 0), level_block(lm_ref, level, 1)], axis=0)
        a_high, a_low = split(full)
        a_both = jnp.concatenate([a_high, a_high], axis=1)
        for q in range(0, cols, LOW):
            lows, highs = [], []
            for s in range(q, q + LOW, boxes):
                v = vals[:, s:s + boxes]
                lows.append(jnp.where(bit, pltpu.roll(v, distance, 1), v))
                highs.append(jnp.where(bit, v, pltpu.roll(v, boxes - distance, 1)))
            stacked = join(jnp.concatenate(lows, axis=1), jnp.concatenate(highs, axis=1))
            s_high, s_low = split(stacked)
            both = jnp.concatenate([s_high, s_low], axis=0)
            mixed = dot(a_both, both) + dot(a_low, s_high)
            for n, s in enumerate(range(q, q + LOW, boxes)):
                part = mixed[:, n * boxes:(n + 1) * boxes]
                vals[:, s:s + boxes] = jnp.where(bit, part[2 * rank:], part[:2 * rank])
    size = cols // CHUNKS
    for n in range(CHUNKS):
        piece = vals[:, n * size:(n + 1) * size]
        outs[n][...] = piece
        outs[CHUNKS + n][...] = piece.astype(BF16)


def cross_kernel(level, bit_index, lm_ref, own_ref, other_ref, *outs):
    upper = (lax.axis_index("tgt") // 2**bit_index) % 2
    block = level_block(lm_ref, level, upper)
    own = own_ref[...]
    other = other_ref[...].astype(F32)
    is_upper = jnp.broadcast_to(upper, own.shape) == 1
    stacked = join(jnp.where(is_upper, other, own), jnp.where(is_upper, own, other))
    mixed = dot3(block, stacked)
    for out in outs:
        out[...] = mixed.astype(out.dtype)


def near_kernel(leaves_ref, tiles_ref, out_ref, wide, weights):
    points, rhs, boxes = leaves_ref.shape
    wide[...] = leaves_ref[...].astype(F32)
    block = 2

    def targets(g, carry):
        for k in range(block):
            for c in range(2):
                weights[2 * k + c] = tiles_ref[c, g * block + k].astype(F32)
        acc = [jnp.zeros((rhs, boxes), F32) for _ in range(2 * block)]
        for j in range(points):
            leaf = wide[j]
            for k in range(2 * block):
                acc[k] = acc[k] + weights[k, pl.ds(j, 1), :] * leaf
        for k in range(block):
            for c in range(2):
                out_ref[c, g * block + k] = acc[2 * k + c]
        return carry

    lax.fori_loop(0, out_ref.shape[1] // block, targets, 0)


def far_kernel(basis_ref, near_ref, *rest):
    coef_refs = rest[:CHUNKS]
    out_ref, coeff, weights = rest[CHUNKS:]
    _, targets_count, rank, boxes = basis_ref.shape
    rhs = out_ref.shape[2]
    sources = coef_refs[0].shape[0]
    per = rhs // sources // CHUNKS
    for s in range(sources):
        for n in range(CHUNKS):
            for h in range(per):
                at = (s * CHUNKS + n) * per + h
                piece = coef_refs[n][s, :, h * boxes:(h + 1) * boxes].astype(F32)
                coeff[pl.ds(at, 2 * rank, stride=rhs), :] = piece
    block = 2

    def targets(g, carry):
        for k in range(block):
            for c in range(2):
                weights[2 * k + c] = basis_ref[c, g * block + k].astype(F32)
        acc = [near_ref[k % 2, g * block + k // 2] for k in range(2 * block)]
        for r in range(rank):
            real = coeff[r * rhs:(r + 1) * rhs, :]
            imag = coeff[(rank + r) * rhs:(rank + r + 1) * rhs, :]
            for k in range(block):
                w_real = weights[2 * k, pl.ds(r, 1), :]
                w_imag = weights[2 * k + 1, pl.ds(r, 1), :]
                acc[2 * k] = acc[2 * k] + w_real * real - w_imag * imag
                acc[2 * k + 1] = acc[2 * k + 1] + w_real * imag + w_imag * real
        for k in range(block):
            for c in range(2):
                out_ref[c, g * block + k] = acc[2 * k + c].astype(BF16)
        return carry

    lax.fori_loop(0, targets_count // block, targets, 0)


def call(body, out_shape, scratch, operands, flops=0, moved=0):
    many = isinstance(out_shape, (list, tuple))
    return pl.pallas_call(
        body,
        out_shape=out_shape,
        in_specs=[VM] * len(operands),
        out_specs=[VM] * len(out_shape) if many else VM,
        scratch_shapes=scratch,
        compiler_params=PARAMS,
        cost_estimate=pl.CostEstimate(flops=flops, bytes_accessed=moved, transcendentals=0),
    )(*operands)


def on_device(sources, leaf_order, skeleton, interp_rows, near_tiles, target_basis, level_maps):
    tgt_count = lax.axis_size("tgt")
    src_count = lax.axis_size("src")
    point_count, rhs = sources.shape
    boxes, rank = skeleton.shape
    leaf = interp_rows.shape[3]
    half = leaf // src_count
    width = rhs // src_count
    cols = width * boxes
    size = cols // CHUNKS
    shape = jax.ShapeDtypeStruct
    vmem = pltpu.VMEM

    index = leaf_order.reshape(boxes, half).T.reshape(point_count // LOW, LOW)
    halves = call(
        gather_kernel, shape((half, rhs, boxes), BF16),
        [vmem((point_count // LOW * rhs, LOW), BF16)], (sources.T, index),
        2 * point_count * rhs * point_count, 2**20,
    )
    leaves = lax.all_gather(halves, "src", axis=0, tiled=True)
    local_levels = boxes.bit_length() - 1
    cross_count = tgt_count.bit_length() - 1
    made = call(
        lambda *refs: local_kernel(local_levels, *refs),
        [shape((2 * rank, size), F32)] * CHUNKS + [shape((2 * rank, size), BF16)] * CHUNKS,
        [
            vmem((leaf, width, boxes), F32), vmem((8, leaf, boxes), F32),
            vmem((2 * rank * width, boxes), F32), vmem((2 * rank, cols), F32),
        ],
        (leaves, skeleton.T, interp_rows.transpose(0, 2, 3, 1), level_maps),
        10**9, 2**22,
    )
    values, narrow = list(made[:CHUNKS]), list(made[CHUNKS:])
    near = call(
        near_kernel, shape((2, half, rhs, boxes), F32),
        [vmem((leaf, rhs, boxes), F32), vmem((4, leaf, boxes), F32)],
        (leaves, near_tiles.transpose(0, 2, 3, 1)),
        5 * 10**9, 2**24,
    )
    for bit_index in range(cross_count):
        last = bit_index == cross_count - 1
        level = local_levels + bit_index
        others = [from_partner(piece, "tgt", bit_index) for piece in narrow]
        for n in range(CHUNKS):
            out = [shape((2 * rank, size), BF16)]
            if not last:
                out.append(shape((2 * rank, size), F32))
            mixed = call(
                lambda *refs: cross_kernel(level, bit_index, *refs), out, [],
                (level_maps, values[n], others[n]), 10**8, 2**20,
            )
            narrow[n] = mixed[0]
            if not last:
                values[n] = mixed[1]
    rounded = [lax.all_gather(piece, "src", axis=0) for piece in narrow]
    field = call(
        far_kernel, shape((2, half, rhs, boxes), BF16),
        [vmem((2 * rank * rhs, boxes), F32), vmem((4, rank, boxes), F32)],
        (target_basis.transpose(0, 2, 3, 1), near, *rounded),
        5 * 10**9, 2**22,
    )
    return field.transpose(0, 3, 1, 2).reshape(2, boxes * half, rhs)


def solution(mesh):
    return jax.shard_map(
        on_device,
        mesh=mesh,
        in_specs=(
            P(("grp", "tgt", "src"), None),
            P(("grp", "tgt", "src")),
            P(("grp", "tgt"), None),
            P(None, ("grp", "tgt"), None, None),
            P(None, ("grp", "tgt"), "src", None),
            P(None, ("grp", "tgt"), "src", None),
            P(None, "grp", None, None, None),
        ),
        out_specs=P(None, ("grp", "tgt", "src"), None),
        check_vma=False,
    )
```

```python
import jax
import jax.numpy as jnp
from jax import lax
from jax.experimental import pallas as pl
from jax.experimental.pallas import tpu as pltpu
from jax.sharding import PartitionSpec as P

F32 = jnp.float32
BF16 = jnp.bfloat16
CHUNKS = 4
LOW = 256
VM = pl.BlockSpec(memory_space=pltpu.VMEM)
PARAMS = pltpu.CompilerParams(vmem_limit_bytes=40 * 2**20)


def gather_kernel(src_ref, idx_ref, out_ref, table):
    rhs, points = src_ref.shape
    high_count = points // LOW
    boxes = out_ref.shape[2]
    per = LOW // boxes
    for high in range(high_count):
        table[pl.ds(high * rhs, rhs), :] = src_ref[:, pl.ds(high * LOW, LOW)]

    def step(g, carry):
        index = idx_ref[pl.ds(g, 1), :]
        low = index % LOW
        high_of = jnp.broadcast_to(index // LOW, (rhs, LOW))
        rows = lax.broadcasted_iota(jnp.int32, (LOW, LOW), 0)
        onehot = jnp.where(rows == low, 1.0, 0.0).astype(BF16)
        found = jnp.dot(table[...], onehot, preferred_element_type=F32)
        total = jnp.zeros((rhs, LOW), F32)
        for high in range(high_count):
            total = jnp.where(high_of == high, found[high * rhs:(high + 1) * rhs], total)
        for part in range(per):
            out_ref[g * per + part] = total[:, part * boxes:(part + 1) * boxes].astype(BF16)
        return carry

    lax.fori_loop(0, idx_ref.shape[0], step, 0)


def split(value):
    high = value.astype(BF16)
    return high, (value - high.astype(F32)).astype(BF16)


def level_block(lm_ref, level, upper):
    real = lm_ref[0, level, upper]
    imag = lm_ref[1, level, upper]
    top = jnp.concatenate([real, -imag], axis=1)
    bottom = jnp.concatenate([imag, real], axis=1)
    return jnp.concatenate([top, bottom], axis=0)


def join(lower, higher):
    half = lower.shape[0] // 2
    return jnp.concatenate([lower[:half], higher[:half], lower[half:], higher[half:]], axis=0)


def dot(a, b):
    return jnp.dot(a, b, preferred_element_type=F32)


def dot3(a, b):
    a_high, a_low = split(a)
    b_high, b_low = split(b)
    return dot(a_high, b_high) + dot(a_high, b_low) + dot(a_low, b_high)


def local_kernel(local_levels, leaves_ref, skel_ref, interp_ref, lm_ref, vals,
                 wide, weights, coeff):
    points, rhs, boxes = leaves_ref.shape
    rank = skel_ref.shape[0]
    width = rhs // lax.axis_size("src")
    start = pl.multiple_of(lax.axis_index("src") * width, width)
    wide[...] = leaves_ref[:, pl.ds(start, width), :].astype(F32)
    block = 4
    rows = lax.broadcasted_iota(jnp.int32, (points, boxes), 0)

    def ranks(g, carry):
        for k in range(block):
            r = g * block + k
            pick = jnp.where(rows == skel_ref[pl.ds(r, 1), :], 1.0, 0.0)
            weights[2 * k] = interp_ref[0, r].astype(F32) + pick
            weights[2 * k + 1] = interp_ref[1, r].astype(F32)
        acc = [jnp.zeros((width, boxes), F32) for _ in range(2 * block)]
        for j in range(points):
            leaf = wide[j]
            for k in range(2 * block):
                acc[k] = acc[k] + weights[k, pl.ds(j, 1), :] * leaf
        for k in range(block):
            for c in range(2):
                at = pl.multiple_of((c * rank + g * block + k) * width, width)
                coeff[pl.ds(at, width), :] = acc[2 * k + c]
        return carry

    lax.fori_loop(0, rank // block, ranks, 0)
    for h in range(width):
        vals[:, h * boxes:(h + 1) * boxes] = coeff[pl.ds(h, 2 * rank, stride=width), :]
    cols = width * boxes
    lane = lax.broadcasted_iota(jnp.int32, (2 * rank, boxes), 1)
    for level in range(local_levels):
        distance = 2**level
        bit = (lane // distance) % 2 == 1
        full = jnp.concatenate([level_block(lm_ref, level, 0), level_block(lm_ref, level, 1)], axis=0)
        a_high, a_low = split(full)
        a_both = jnp.concatenate([a_high, a_high], axis=1)
        for q in range(0, cols, LOW):
            lows, highs = [], []
            for s in range(q, q + LOW, boxes):
                v = vals[:, s:s + boxes]
                lows.append(jnp.where(bit, pltpu.roll(v, distance, 1), v))
                highs.append(jnp.where(bit, v, pltpu.roll(v, boxes - distance, 1)))
            stacked = join(jnp.concatenate(lows, axis=1), jnp.concatenate(highs, axis=1))
            s_high, s_low = split(stacked)
            both = jnp.concatenate([s_high, s_low], axis=0)
            mixed = dot(a_both, both) + dot(a_low, s_high)
            for n, s in enumerate(range(q, q + LOW, boxes)):
                part = mixed[:, n * boxes:(n + 1) * boxes]
                vals[:, s:s + boxes] = jnp.where(bit, part[2 * rank:], part[:2 * rank])


def partner_of(axis, bit_index):
    me = lax.axis_index(axis)
    mask = 2**bit_index
    return {axis: me + mask - 2 * mask * ((me // mask) % 2)}


def plan(bit_count):
    steps = [(bit, n) for bit in range(bit_count) for n in range(CHUNKS)]
    return sorted(steps, key=lambda at: at[1] + 1.5 * at[0] + (at[0] == bit_count - 1))


def cross_kernel(local_levels, bit_count, lm_ref, vals_ref, leaves_ref, tiles_ref, basis_ref, out_ref,
                 vals, sent, came, mine, theirs, wide, weights, near, basis, coeff, send_sem, recv_sem):
    points, rhs, boxes = leaves_ref.shape
    _, target_count, rank, _ = basis_ref.shape
    size = sent.shape[3]
    per = size // boxes
    group = coeff.shape[1] // (2 * rank)
    sources = group // per
    src_first = jnp.broadcast_to(lax.axis_index("src"), (2 * rank, size)) == 0

    barrier = pltpu.get_barrier_semaphore()
    peers = [partner_of("tgt", bit) for bit in range(bit_count)] + [partner_of("src", 0)]
    for peer in peers:
        pl.semaphore_signal(barrier, inc=1, device_id=peer, device_id_type=pl.DeviceIdType.MESH)
    pl.semaphore_wait(barrier, len(peers))

    def copy_of(bit, n):
        inside = bit < bit_count
        return pltpu.make_async_remote_copy(
            src_ref=sent.at[bit, n] if inside else mine.at[n],
            dst_ref=came.at[bit, n] if inside else theirs.at[n],
            send_sem=send_sem.at[bit, n],
            recv_sem=recv_sem.at[bit, n],
            device_id=peers[bit],
            device_id_type=pl.DeviceIdType.MESH,
        )

    for n in range(CHUNKS):
        piece = vals_ref[:, n * size:(n + 1) * size]
        sent[0, n] = piece.astype(BF16)
        copy_of(0, n).start()
        vals[n] = piece

    for n in range(CHUNKS):
        for s in range(sources):
            start = s * per * CHUNKS + n * per
            wide[:, n * group + s * per:n * group + (s + 1) * per, :] = (
                leaves_ref[...].astype(F32)[:, start:start + per, :]
            )

    block = weights.shape[0] // 2

    def near_step(g, carry):
        for k in range(block):
            for c in range(2):
                weights[2 * k + c] = tiles_ref[c, g * block + k].astype(F32)
        acc = jnp.zeros((2 * block, rhs, boxes), F32)
        for j in range(points):
            acc = acc + weights[:, j:j + 1, :] * wide[j][None]
        for k in range(block):
            for c in range(2):
                for n in range(CHUNKS):
                    near[n, c, g * block + k] = acc[2 * k + c, n * group:(n + 1) * group]
        return carry

    near_total = target_count // block
    done = 0

    def near_part(count):
        nonlocal done
        end = min(near_total, done + count)
        if end > done:
            lax.fori_loop(done, end, near_step, 0)
        done = end

    def far_part(n):
        copy_of(bit_count, n).wait_recv()
        own = mine[n].astype(F32)
        other = theirs[n].astype(F32)
        for s, piece in enumerate((jnp.where(src_first, own, other), jnp.where(src_first, other, own))):
            for h in range(per):
                coeff[n, pl.ds(s * per + h, 2 * rank, stride=group), :] = piece[:, h * boxes:(h + 1) * boxes]
        many = 8

        def far_step(g, carry):
            rows = pl.ds(pl.multiple_of(g * many, many), many)
            real_acc = near[n, 0, rows]
            imag_acc = near[n, 1, rows]
            for r in range(rank):
                real = coeff[n, r * group:(r + 1) * group, :][None]
                imag = coeff[n, (rank + r) * group:(rank + r + 1) * group, :][None]
                w_real = basis[0, rows, r:r + 1, :]
                w_imag = basis[1, rows, r:r + 1, :]
                real_acc = real_acc + w_real * real - w_imag * imag
                imag_acc = imag_acc + w_real * imag + w_imag * real
            out_ref[n, 0, rows] = real_acc.astype(BF16)
            out_ref[n, 1, rows] = imag_acc.astype(BF16)
            return carry

        lax.fori_loop(0, target_count // many, far_step, 0)

    slots = [6, 3, 3, 2, 2]
    for at, (bit, n) in enumerate(plan(bit_count)):
        last = bit == bit_count - 1
        if last and n == 0:
            near_part(near_total)
            basis[...] = basis_ref[...].astype(F32)
        elif at < len(slots):
            near_part(slots[at])
        copy_of(bit, n).wait_recv()
        upper = (lax.axis_index("tgt") // 2**bit) % 2
        own = vals[n]
        other = came[bit, n].astype(F32)
        is_upper = jnp.broadcast_to(upper, own.shape) == 1
        stacked = join(jnp.where(is_upper, other, own), jnp.where(is_upper, own, other))
        mixed = dot3(level_block(lm_ref, local_levels + bit, upper), stacked)
        if last:
            mine[n] = mixed.astype(BF16)
        else:
            vals[n] = mixed
            sent[bit + 1, n] = mixed.astype(BF16)
        copy_of(bit + 1, n).start()
        if last:
            far_part(n)
    for bit in range(bit_count + 1):
        for n in range(CHUNKS):
            copy_of(bit, n).wait_send()


def call(body, out_shape, scratch, operands, params=PARAMS):
    return pl.pallas_call(
        body,
        out_shape=out_shape,
        in_specs=[VM] * len(operands),
        out_specs=VM,
        scratch_shapes=scratch,
        compiler_params=params,
    )(*operands)


def on_device(sources, leaf_order, skeleton, interp_rows, near_tiles, target_basis, level_maps):
    tgt_count = lax.axis_size("tgt")
    src_count = lax.axis_size("src")
    point_count, rhs = sources.shape
    boxes, rank = skeleton.shape
    leaf = interp_rows.shape[3]
    half = leaf // src_count
    width = rhs // src_count
    cols = width * boxes
    size = cols // CHUNKS
    shape = jax.ShapeDtypeStruct
    vmem = pltpu.VMEM

    index = leaf_order.reshape(boxes, half).T.reshape(point_count // LOW, LOW)
    halves = call(
        gather_kernel, shape((half, rhs, boxes), BF16),
        [vmem((point_count // LOW * rhs, LOW), BF16)], (sources.T, index),
    )
    leaves = lax.all_gather(halves, "src", axis=0, tiled=True)
    local_levels = boxes.bit_length() - 1
    cross_count = tgt_count.bit_length() - 1
    values = call(
        lambda *refs: local_kernel(local_levels, *refs),
        shape((2 * rank, cols), F32),
        [
            vmem((leaf, width, boxes), F32), vmem((8, leaf, boxes), F32),
            vmem((2 * rank * width, boxes), F32),
        ],
        (leaves, skeleton.T, interp_rows.transpose(0, 2, 3, 1), level_maps),
    )
    group = rhs // CHUNKS
    field = call(
        lambda *refs: cross_kernel(local_levels, cross_count, *refs),
        shape((CHUNKS, 2, half, group, boxes), BF16),
        [
            vmem((CHUNKS, 2 * rank, size), F32),
            vmem((cross_count, CHUNKS, 2 * rank, size), BF16),
            vmem((cross_count, CHUNKS, 2 * rank, size), BF16),
            vmem((CHUNKS, 2 * rank, size), BF16),
            vmem((CHUNKS, 2 * rank, size), BF16),
            vmem((leaf, rhs, boxes), F32),
            vmem((4, leaf, boxes), F32),
            vmem((CHUNKS, 2, half, group, boxes), F32),
            vmem((2, half, rank, boxes), F32),
            vmem((CHUNKS, 2 * rank * group, boxes), F32),
            pltpu.SemaphoreType.DMA((cross_count + 1, CHUNKS)),
            pltpu.SemaphoreType.DMA((cross_count + 1, CHUNKS)),
        ],
        (level_maps, values, leaves, near_tiles.transpose(0, 2, 3, 1), target_basis.transpose(0, 2, 3, 1)),
        pltpu.CompilerParams(vmem_limit_bytes=40 * 2**20, collective_id=0, has_side_effects=True),
    )
    field = field.reshape(CHUNKS, 2, half, src_count, group // src_count, boxes)
    return field.transpose(1, 5, 2, 3, 0, 4).reshape(2, boxes * half, rhs)


def solution(mesh):
    return jax.shard_map(
        on_device,
        mesh=mesh,
        in_specs=(
            P(("grp", "tgt", "src"), None),
            P(("grp", "tgt", "src")),
            P(("grp", "tgt"), None),
            P(None, ("grp", "tgt"), None, None),
            P(None, ("grp", "tgt"), "src", None),
            P(None, ("grp", "tgt"), "src", None),
            P(None, "grp", None, None, None),
        ),
        out_specs=P(None, ("grp", "tgt", "src"), None),
        check_vma=False,
    )
```

```python
import jax
import jax.numpy as jnp
from jax import lax
from jax.experimental import pallas as pl
from jax.experimental.pallas import tpu as pltpu
from jax.sharding import PartitionSpec as P

F32 = jnp.float32
BF16 = jnp.bfloat16
CHUNKS = 4
LOW = 256
def split(value):
    high = value.astype(BF16)
    return high, (value - high.astype(F32)).astype(BF16)


def level_block(lm_ref, level, upper):
    real = lm_ref[0, level, upper]
    imag = lm_ref[1, level, upper]
    top = jnp.concatenate([real, -imag], axis=1)
    bottom = jnp.concatenate([imag, real], axis=1)
    return jnp.concatenate([top, bottom], axis=0)


def join(lower, higher):
    half = lower.shape[0] // 2
    return jnp.concatenate([lower[:half], higher[:half], lower[half:], higher[half:]], axis=0)


def dot(a, b):
    return jnp.dot(a, b, preferred_element_type=F32)


def dot3(a, b):
    a_high, a_low = split(a)
    b_high, b_low = split(b)
    return dot(a_high, b_high) + dot(a_high, b_low) + dot(a_low, b_high)


def partner_of(axis, bit_index):
    me = lax.axis_index(axis)
    mask = 2**bit_index
    return {axis: me + mask - 2 * mask * ((me // mask) % 2)}


def plan(bit_count):
    steps = [(bit, n) for bit in range(bit_count) for n in range(CHUNKS)]
    return sorted(steps, key=lambda at: at[1] + 1.5 * at[0] + (at[0] == bit_count - 1))


def column_index(order, rhs_rows):
    rows, lanes = order.shape
    turned = order.astype(F32).T.astype(BF16)
    per = lanes // rhs_rows
    at_row = lax.broadcasted_iota(jnp.int32, (rows, rows * per), 0)
    at_lane = lax.broadcasted_iota(jnp.int32, (rows, rows * per), 1)
    total = jnp.zeros((rhs_rows, rows * per), F32)
    for k in range(per):
        place = jnp.where(at_lane == at_row * per + k, 1.0, 0.0).astype(BF16)
        total = total + dot(turned[k * rhs_rows:(k + 1) * rhs_rows], place)
    return total.astype(jnp.int32)


def kernel(local_levels, bit_count, sources_hbm, order_hbm, skel_hbm, interp_hbm, tiles_hbm, basis_hbm, maps_hbm,
           out_ref,
           src_ref, order_ref, skel_ref, interp_ref, tiles_ref, basis_ref, lm_ref,
           table, low_ref, high_ref, halves, others, own_wide, weights, coeff_rows, maps_both, maps_low,
           vals, sent, came, mine, theirs, wide, near, basis, coeff, turned,
           in_sem, send_sem, recv_sem, half_send, half_recv):
    half, rhs, boxes = halves.shape
    points = wide.shape[0]
    rank = skel_ref.shape[0]
    size = vals.shape[2]
    per = size // boxes
    group = rhs // CHUNKS
    sources = group // per
    width = rhs // sources
    my_src = lax.axis_index("src")

    pairs = (
        (sources_hbm, src_ref), (order_hbm, order_ref), (maps_hbm, lm_ref), (skel_hbm, skel_ref),
        (interp_hbm, interp_ref), (tiles_hbm, tiles_ref), (basis_hbm, basis_ref),
    )
    loads = [pltpu.make_async_copy(a, b, in_sem.at[k]) for k, (a, b) in enumerate(pairs)]
    for load in loads:
        load.start()

    barrier = pltpu.get_barrier_semaphore()
    peers = [partner_of("tgt", bit) for bit in range(bit_count)] + [partner_of("src", 0)]
    for peer in peers:
        pl.semaphore_signal(barrier, inc=1, device_id=peer, device_id_type=pl.DeviceIdType.MESH)

    loads[1].wait()
    order = order_ref[...]
    low_ref[...] = column_index(order % LOW, half)
    high_ref[...] = column_index(order // LOW, half)
    loads[0].wait()
    high_count = src_ref.shape[1] // LOW
    for high in range(high_count):
        table[pl.ds(high * rhs, rhs), :] = src_ref[:, pl.ds(high * LOW, LOW)]
    together = LOW // boxes

    def gather_step(g, carry):
        low = jnp.concatenate([low_ref[pl.ds(g * together + k, 1), :] for k in range(together)], axis=1)
        high_at = jnp.concatenate([high_ref[pl.ds(g * together + k, 1), :] for k in range(together)], axis=1)
        high_of = jnp.broadcast_to(high_at, (rhs, LOW))
        rows = lax.broadcasted_iota(jnp.int32, (LOW, LOW), 0)
        onehot = jnp.where(rows == low, 1.0, 0.0).astype(BF16)
        found = dot(table[...], onehot)
        total = jnp.zeros((rhs, LOW), F32)
        for high in range(high_count):
            total = jnp.where(high_of == high, found[high * rhs:(high + 1) * rhs], total)
        for k in range(together):
            halves[g * together + k] = total[:, k * boxes:(k + 1) * boxes].astype(BF16)
        return carry

    pieces = 2
    piece_rows = half // pieces

    def half_copy(k):
        return pltpu.make_async_remote_copy(
            src_ref=halves.at[pl.ds(k * piece_rows, piece_rows)],
            dst_ref=others.at[pl.ds(k * piece_rows, piece_rows)],
            send_sem=half_send.at[k],
            recv_sem=half_recv.at[k],
            device_id=peers[bit_count],
            device_id_type=pl.DeviceIdType.MESH,
        )

    steps = piece_rows // together
    for k in range(pieces):
        lax.fori_loop(k * steps, (k + 1) * steps, gather_step, 0)
        if k == 0:
            pl.semaphore_wait(barrier, len(peers))
        half_copy(k).start()

    loads[2].wait()
    for level in range(local_levels):
        full = jnp.concatenate([level_block(lm_ref, level, 0), level_block(lm_ref, level, 1)], axis=0)
        a_high, a_low = split(full)
        maps_both[level] = jnp.concatenate([a_high, a_high], axis=1)
        maps_low[level] = a_low

    def spread(ref, at):
        rows = pl.ds(pl.multiple_of(at * half, half), half)
        own_wide[rows] = ref[:, pl.ds(pl.multiple_of(my_src * width, width), width), :].astype(F32)
        for n in range(CHUNKS):
            for s in range(sources):
                start = s * width + n * per
                wide[rows, n * group + s * per:n * group + (s + 1) * per, :] = (
                    ref[...].astype(F32)[:, start:start + per, :]
                )

    spread(halves, my_src)
    for k in range(pieces):
        half_copy(k).wait_recv()
    spread(others, 1 - my_src)

    loads[3].wait()
    loads[4].wait()
    block = weights.shape[0] // 2
    leaf_rows = lax.broadcasted_iota(jnp.int32, (points, boxes), 0)

    def rank_step(g, carry):
        for k in range(block):
            r = g * block + k
            pick = jnp.where(leaf_rows == skel_ref[pl.ds(r, 1), :], 1.0, 0.0)
            weights[2 * k] = interp_ref[0, r].astype(F32) + pick
            weights[2 * k + 1] = interp_ref[1, r].astype(F32)
        acc = jnp.zeros((2 * block, width, boxes), F32)
        for j in range(points):
            acc = acc + weights[:, j:j + 1, :] * own_wide[j][None]
        for k in range(block):
            for c in range(2):
                at = pl.multiple_of((c * rank + g * block + k) * width, width)
                coeff_rows[pl.ds(at, width), :] = acc[2 * k + c]
        return carry

    lax.fori_loop(0, rank // block, rank_step, 0)

    def copy_of(bit, n):
        inside = bit < bit_count
        return pltpu.make_async_remote_copy(
            src_ref=sent.at[bit, n] if inside else mine.at[n],
            dst_ref=came.at[bit, n] if inside else theirs.at[n],
            send_sem=send_sem.at[bit, n],
            recv_sem=recv_sem.at[bit, n],
            device_id=peers[bit],
            device_id_type=pl.DeviceIdType.MESH,
        )

    lane = lax.broadcasted_iota(jnp.int32, (2 * rank, boxes), 1)
    for first in range(0, CHUNKS, 2):
        chunks = range(first, min(first + 2, CHUNKS))
        for n in chunks:
            for h in range(per):
                vals[n, :, h * boxes:(h + 1) * boxes] = coeff_rows[pl.ds(n * per + h, 2 * rank, stride=width), :]
        for level in range(local_levels):
            distance = 2**level
            bit = (lane // distance) % 2 == 1
            for n in chunks:
                for q in range(0, size, LOW):
                    lows, highs = [], []
                    for at in range(q, q + LOW, boxes):
                        v = vals[n, :, at:at + boxes]
                        lows.append(jnp.where(bit, pltpu.roll(v, distance, 1), v))
                        highs.append(jnp.where(bit, v, pltpu.roll(v, boxes - distance, 1)))
                    stacked = join(jnp.concatenate(lows, axis=1), jnp.concatenate(highs, axis=1))
                    s_high, s_low = split(stacked)
                    both = jnp.concatenate([s_high, s_low], axis=0)
                    mixed = dot(maps_both[level], both) + dot(maps_low[level], s_high)
                    for k, at in enumerate(range(q, q + LOW, boxes)):
                        piece = mixed[:, k * boxes:(k + 1) * boxes]
                        vals[n, :, at:at + boxes] = jnp.where(bit, piece[2 * rank:], piece[:2 * rank])
        for n in chunks:
            sent[0, n] = vals[n].astype(BF16)
            copy_of(0, n).start()

    near_block = 2
    loads[5].wait()

    def near_step(g, carry):
        for k in range(near_block):
            for c in range(2):
                weights[2 * k + c] = tiles_ref[c, g * near_block + k].astype(F32)
        acc = jnp.zeros((2 * near_block, rhs, boxes), F32)
        for j in range(points):
            acc = acc + weights[:2 * near_block, j:j + 1, :] * wide[j][None]
        for k in range(near_block):
            for c in range(2):
                for n in range(CHUNKS):
                    at = pl.multiple_of((g * near_block + k) * group, group)
                    near[n, c, pl.ds(at, group), :] = acc[2 * k + c, n * group:(n + 1) * group]
        return carry

    near_total = half // near_block
    done = 0

    def near_part(count):
        nonlocal done
        end = min(near_total, done + count)
        if end > done:
            lax.fori_loop(done, end, near_step, 0)
        done = end

    src_first = jnp.broadcast_to(my_src, (2 * rank, size)) == 0
    box_of = lax.broadcasted_iota(jnp.int32, (half, boxes), 1)
    fold = boxes // half
    gathered = jnp.where(
        lax.broadcasted_iota(jnp.int32, (half, boxes), 0) == box_of // fold, 1.0, 0.0
    ).astype(BF16)

    def far_part(n):
        copy_of(bit_count, n).wait_recv()
        own = mine[n].astype(F32)
        other = theirs[n].astype(F32)
        for s, piece in enumerate((jnp.where(src_first, own, other), jnp.where(src_first, other, own))):
            for h in range(per):
                coeff[n, pl.ds(s * per + h, 2 * rank, stride=group), :] = piece[:, h * boxes:(h + 1) * boxes]
        many = 8

        def far_step(g, carry):
            rows = pl.ds(pl.multiple_of(g * many, many), many)
            flat = pl.ds(pl.multiple_of(g * many * group, many * group), many * group)
            real_acc = near[n, 0, flat, :].reshape(many, group, boxes)
            imag_acc = near[n, 1, flat, :].reshape(many, group, boxes)
            for r in range(rank):
                real = coeff[n, r * group:(r + 1) * group, :][None]
                imag = coeff[n, (rank + r) * group:(rank + r + 1) * group, :][None]
                w_real = basis[0, rows, r:r + 1, :]
                w_imag = basis[1, rows, r:r + 1, :]
                real_acc = real_acc + w_real * real - w_imag * imag
                imag_acc = imag_acc + w_real * imag + w_imag * real
            near[n, 0, flat, :] = real_acc.reshape(many * group, boxes)
            near[n, 1, flat, :] = imag_acc.reshape(many * group, boxes)
            return carry

        lax.fori_loop(0, half // many, far_step, 0)
        for c in range(2):
            for s in range(sources):
                for h in range(per):
                    plane = near[n, c, pl.ds(s * per + h, half, stride=group), :]
                    masked = [jnp.where(box_of % fold == k, plane, 0.0).astype(BF16) for k in range(fold)]
                    moved = lax.dot_general(
                        gathered, jnp.concatenate(masked, axis=0), (((1,), (1,)), ((), ())),
                        preferred_element_type=F32,
                    )
                    at = (s * width + n * per + h) * half
                    turned[c, at:at + half, :] = moved

    slots = [5, 3, 3, 2, 2]
    for at, (bit, n) in enumerate(plan(bit_count)):
        last = bit == bit_count - 1
        if last and n == 0:
            near_part(near_total)
            loads[6].wait()
            basis[...] = basis_ref[...].astype(F32)
        elif at < len(slots):
            near_part(slots[at])
        copy_of(bit, n).wait_recv()
        upper = (lax.axis_index("tgt") // 2**bit) % 2
        own = vals[n]
        other = came[bit, n].astype(F32)
        is_upper = jnp.broadcast_to(upper, own.shape) == 1
        stacked = join(jnp.where(is_upper, other, own), jnp.where(is_upper, own, other))
        mixed = dot3(level_block(lm_ref, local_levels + bit, upper), stacked)
        if last:
            mine[n] = mixed.astype(BF16)
        else:
            vals[n] = mixed
            sent[bit + 1, n] = mixed.astype(BF16)
        copy_of(bit + 1, n).start()
        if last:
            far_part(n)
    lanes = fold * half
    for c in range(2):
        for t in range(half):
            out_ref[c, :, t * lanes:(t + 1) * lanes] = turned[c, pl.ds(t, rhs, stride=half), :].astype(BF16)
    for k in range(pieces):
        half_copy(k).wait_send()
    for bit in range(bit_count + 1):
        for n in range(CHUNKS):
            copy_of(bit, n).wait_send()


def on_device(sources, leaf_order, skeleton, interp_rows, near_tiles, target_basis, level_maps):
    tgt_count = lax.axis_size("tgt")
    src_count = lax.axis_size("src")
    point_count, rhs = sources.shape
    boxes, rank = skeleton.shape
    leaf = interp_rows.shape[3]
    half = leaf // src_count
    width = rhs // src_count
    size = width * boxes // CHUNKS
    group = rhs // CHUNKS
    local_levels = boxes.bit_length() - 1
    bits = tgt_count.bit_length() - 1
    operands = (
        sources.T, leaf_order.reshape(point_count // boxes, boxes), skeleton.T,
        interp_rows.transpose(0, 2, 3, 1), near_tiles.transpose(0, 2, 3, 1),
        target_basis.transpose(0, 2, 3, 1), level_maps,
    )
    vmem = pltpu.VMEM
    dma = pltpu.SemaphoreType.DMA
    field = pl.pallas_call(
        lambda *refs: kernel(local_levels, bits, *refs),
        out_shape=jax.ShapeDtypeStruct((2, rhs, point_count), BF16),
        in_specs=[pl.BlockSpec(memory_space=pl.ANY)] * len(operands),
        out_specs=pl.BlockSpec(memory_space=pltpu.VMEM),
        scratch_shapes=[vmem(operand.shape, operand.dtype) for operand in operands] + [
            vmem((point_count // LOW * rhs, LOW), BF16),
            vmem((half, boxes), jnp.int32),
            vmem((half, boxes), jnp.int32),
            vmem((half, rhs, boxes), BF16),
            vmem((half, rhs, boxes), BF16),
            vmem((leaf, width, boxes), F32),
            vmem((8, leaf, boxes), F32),
            vmem((2 * rank * width, boxes), F32),
            vmem((local_levels, 4 * rank, 8 * rank), BF16),
            vmem((local_levels, 4 * rank, 4 * rank), BF16),
            vmem((CHUNKS, 2 * rank, size), F32),
            vmem((bits, CHUNKS, 2 * rank, size), BF16),
            vmem((bits, CHUNKS, 2 * rank, size), BF16),
            vmem((CHUNKS, 2 * rank, size), BF16),
            vmem((CHUNKS, 2 * rank, size), BF16),
            vmem((leaf, rhs, boxes), F32),
            vmem((CHUNKS, 2, half * group, boxes), F32),
            vmem((2, half, rank, boxes), F32),
            vmem((CHUNKS, 2 * rank * group, boxes), F32),
            vmem((2, rhs * half, boxes), F32),
            dma((len(operands),)),
            dma((bits + 1, CHUNKS)),
            dma((bits + 1, CHUNKS)),
            dma((2,)),
            dma((2,)),
        ],
        compiler_params=pltpu.CompilerParams(
            vmem_limit_bytes=60 * 2**20, collective_id=0, has_side_effects=True
        ),
    )(*operands)
    return field.transpose(0, 2, 1)


def solution(mesh):
    return jax.shard_map(
        on_device,
        mesh=mesh,
        in_specs=(
            P(("grp", "tgt", "src"), None),
            P(("grp", "tgt", "src")),
            P(("grp", "tgt"), None),
            P(None, ("grp", "tgt"), None, None),
            P(None, ("grp", "tgt"), "src", None),
            P(None, ("grp", "tgt"), "src", None),
            P(None, "grp", None, None, None),
        ),
        out_specs=P(None, ("grp", "tgt", "src"), None),
        check_vma=False,
    )
```

```python
import jax
import jax.numpy as jnp
from jax import lax
from jax.experimental import pallas as pl
from jax.experimental.pallas import tpu as pltpu
from jax.sharding import PartitionSpec as P

F32 = jnp.float32
BF16 = jnp.bfloat16
CHUNKS = 4
LOW = 256
def split(value):
    high = value.astype(BF16)
    return high, (value - high.astype(F32)).astype(BF16)


def level_block(lm_ref, level, upper):
    real = lm_ref[0, level, upper]
    imag = lm_ref[1, level, upper]
    top = jnp.concatenate([real, -imag], axis=1)
    bottom = jnp.concatenate([imag, real], axis=1)
    return jnp.concatenate([top, bottom], axis=0)


def join(lower, higher):
    half = lower.shape[0] // 2
    return jnp.concatenate([lower[:half], higher[:half], lower[half:], higher[half:]], axis=0)


def dot(a, b):
    return jnp.dot(a, b, preferred_element_type=F32)


def partner_of(axis, bit_index):
    me = lax.axis_index(axis)
    mask = 2**bit_index
    return {axis: me + mask - 2 * mask * ((me // mask) % 2)}


def plan(bit_count):
    steps = [(bit, n) for bit in range(bit_count) for n in range(CHUNKS)]
    return sorted(steps, key=lambda at: at[1] + 1.5 * at[0] + (at[0] == bit_count - 1))


def column_index(order, rhs_rows):
    rows, lanes = order.shape
    turned = order.astype(F32).T.astype(BF16)
    per = lanes // rhs_rows
    at_row = lax.broadcasted_iota(jnp.int32, (rows, rows * per), 0)
    at_lane = lax.broadcasted_iota(jnp.int32, (rows, rows * per), 1)
    total = jnp.zeros((rhs_rows, rows * per), F32)
    for k in range(per):
        place = jnp.where(at_lane == at_row * per + k, 1.0, 0.0).astype(BF16)
        total = total + dot(turned[k * rhs_rows:(k + 1) * rhs_rows], place)
    return total.astype(jnp.int32)


def kernel(local_levels, bit_count, sources_hbm, order_hbm, skel_hbm, interp_hbm, tiles_hbm, basis_hbm, maps_hbm,
           out_ref,
           src_ref, order_ref, skel_ref, interp_ref, tiles_ref, basis_ref, lm_ref,
           table, low_ref, high_ref, halves, others, own_wide, weights, coeff_rows, maps_both, maps_low, cross_high, cross_low,
           vals, sent, came, mine, theirs, wide, near, basis, coeff, turned,
           in_sem, send_sem, recv_sem, half_send, half_recv):
    half, rhs, boxes = halves.shape
    points = wide.shape[0]
    rank = skel_ref.shape[0]
    size = vals.shape[2]
    per = size // boxes
    group = rhs // CHUNKS
    sources = group // per
    width = rhs // sources
    my_src = lax.axis_index("src")

    pairs = (
        (sources_hbm, src_ref), (order_hbm, order_ref), (maps_hbm, lm_ref), (skel_hbm, skel_ref),
        (interp_hbm, interp_ref), (tiles_hbm, tiles_ref), (basis_hbm, basis_ref),
    )
    loads = [pltpu.make_async_copy(a, b, in_sem.at[k]) for k, (a, b) in enumerate(pairs)]
    for load in loads:
        load.start()

    barrier = pltpu.get_barrier_semaphore()
    peers = [partner_of("tgt", bit) for bit in range(bit_count)] + [partner_of("src", 0)]
    for peer in peers:
        pl.semaphore_signal(barrier, inc=1, device_id=peer, device_id_type=pl.DeviceIdType.MESH)

    loads[1].wait()
    order = order_ref[...]
    low_ref[...] = column_index(order % LOW, half)
    high_ref[...] = column_index(order // LOW, half)
    loads[0].wait()
    high_count = src_ref.shape[1] // LOW
    for high in range(high_count):
        table[pl.ds(high * rhs, rhs), :] = src_ref[:, pl.ds(high * LOW, LOW)]
    together = LOW // boxes

    def gather_step(g, carry):
        low = jnp.concatenate([low_ref[pl.ds(g * together + k, 1), :] for k in range(together)], axis=1)
        high_at = jnp.concatenate([high_ref[pl.ds(g * together + k, 1), :] for k in range(together)], axis=1)
        high_of = jnp.broadcast_to(high_at, (rhs, LOW))
        rows = lax.broadcasted_iota(jnp.int32, (LOW, LOW), 0)
        onehot = jnp.where(rows == low, 1.0, 0.0).astype(BF16)
        found = dot(table[...], onehot)
        total = jnp.zeros((rhs, LOW), F32)
        for high in range(high_count):
            total = jnp.where(high_of == high, found[high * rhs:(high + 1) * rhs], total)
        for k in range(together):
            halves[g * together + k] = total[:, k * boxes:(k + 1) * boxes].astype(BF16)
        return carry

    pieces = 2
    piece_rows = half // pieces

    def half_copy(k):
        return pltpu.make_async_remote_copy(
            src_ref=halves.at[pl.ds(k * piece_rows, piece_rows)],
            dst_ref=others.at[pl.ds(k * piece_rows, piece_rows)],
            send_sem=half_send.at[k],
            recv_sem=half_recv.at[k],
            device_id=peers[bit_count],
            device_id_type=pl.DeviceIdType.MESH,
        )

    steps = piece_rows // together
    for k in range(pieces):
        lax.fori_loop(k * steps, (k + 1) * steps, gather_step, 0)
        if k == 0:
            pl.semaphore_wait(barrier, len(peers))
        half_copy(k).start()

    loads[2].wait()
    for level in range(local_levels):
        full = jnp.concatenate([level_block(lm_ref, level, 0), level_block(lm_ref, level, 1)], axis=0)
        a_high, a_low = split(full)
        maps_both[level] = jnp.concatenate([a_high, a_high], axis=1)
        maps_low[level] = a_low

    for bit in range(bit_count):
        upper = (lax.axis_index("tgt") // 2**bit) % 2
        cross_high[bit], cross_low[bit] = split(level_block(lm_ref, local_levels + bit, upper))

    def spread(ref, at):
        rows = pl.ds(pl.multiple_of(at * half, half), half)
        own_wide[rows] = ref[:, pl.ds(pl.multiple_of(my_src * width, width), width), :].astype(F32)
        for n in range(CHUNKS):
            for s in range(sources):
                start = s * width + n * per
                wide[rows, n * group + s * per:n * group + (s + 1) * per, :] = (
                    ref[...].astype(F32)[:, start:start + per, :]
                )

    spread(halves, my_src)
    for k in range(pieces):
        half_copy(k).wait_recv()
    spread(others, 1 - my_src)

    loads[3].wait()
    loads[4].wait()
    block = weights.shape[0] // 2
    leaf_rows = lax.broadcasted_iota(jnp.int32, (points, boxes), 0)

    def rank_step(g, carry):
        for k in range(block):
            r = g * block + k
            pick = jnp.where(leaf_rows == skel_ref[pl.ds(r, 1), :], 1.0, 0.0)
            weights[2 * k] = interp_ref[0, r].astype(F32) + pick
            weights[2 * k + 1] = interp_ref[1, r].astype(F32)
        acc = jnp.zeros((2 * block, width, boxes), F32)
        for j in range(points):
            acc = acc + weights[:, j:j + 1, :] * own_wide[j][None]
        for k in range(block):
            for c in range(2):
                at = pl.multiple_of((c * rank + g * block + k) * width, width)
                coeff_rows[pl.ds(at, width), :] = acc[2 * k + c]
        return carry

    lax.fori_loop(0, rank // block, rank_step, 0)

    def copy_of(bit, n):
        inside = bit < bit_count
        return pltpu.make_async_remote_copy(
            src_ref=sent.at[bit, n] if inside else mine.at[n],
            dst_ref=came.at[bit, n] if inside else theirs.at[n],
            send_sem=send_sem.at[bit, n],
            recv_sem=recv_sem.at[bit, n],
            device_id=peers[bit],
            device_id_type=pl.DeviceIdType.MESH,
        )

    lane = lax.broadcasted_iota(jnp.int32, (2 * rank, boxes), 1)
    for first in range(0, CHUNKS, 2):
        chunks = range(first, min(first + 2, CHUNKS))
        for n in chunks:
            for h in range(per):
                vals[n, :, h * boxes:(h + 1) * boxes] = coeff_rows[pl.ds(n * per + h, 2 * rank, stride=width), :]
        for level in range(local_levels):
            distance = 2**level
            bit = (lane // distance) % 2 == 1
            for n in chunks:
                for q in range(0, size, LOW):
                    lows, highs = [], []
                    for at in range(q, q + LOW, boxes):
                        v = vals[n, :, at:at + boxes]
                        lows.append(jnp.where(bit, pltpu.roll(v, distance, 1), v))
                        highs.append(jnp.where(bit, v, pltpu.roll(v, boxes - distance, 1)))
                    stacked = join(jnp.concatenate(lows, axis=1), jnp.concatenate(highs, axis=1))
                    s_high, s_low = split(stacked)
                    both = jnp.concatenate([s_high, s_low], axis=0)
                    mixed = dot(maps_both[level], both) + dot(maps_low[level], s_high)
                    for k, at in enumerate(range(q, q + LOW, boxes)):
                        piece = mixed[:, k * boxes:(k + 1) * boxes]
                        vals[n, :, at:at + boxes] = jnp.where(bit, piece[2 * rank:], piece[:2 * rank])
        for n in chunks:
            sent[0, n] = vals[n].astype(BF16)
            copy_of(0, n).start()

    near_block = 2
    loads[5].wait()
    near[...] = jnp.zeros(near.shape, F32)

    def near_step(g, carry):
        for k in range(near_block):
            for c in range(2):
                weights[2 * k + c] = tiles_ref[c, g * near_block + k].astype(F32)
        acc = jnp.zeros((2 * near_block, rhs, boxes), F32)
        for j in range(points):
            acc = acc + weights[:2 * near_block, j:j + 1, :] * wide[j][None]
        for k in range(near_block):
            for c in range(2):
                for n in range(CHUNKS):
                    at = pl.multiple_of((g * near_block + k) * group, group)
                    rows = pl.ds(at, group)
                    near[n, c, rows, :] = near[n, c, rows, :] + acc[2 * k + c, n * group:(n + 1) * group]
        return carry

    near_total = half // near_block
    done = 0

    def near_part(count):
        nonlocal done
        end = min(near_total, done + count)
        if end > done:
            lax.fori_loop(done, end, near_step, 0)
        done = end

    src_first = jnp.broadcast_to(my_src, (2 * rank, size)) == 0
    box_of = lax.broadcasted_iota(jnp.int32, (half, boxes), 1)
    fold = boxes // half
    gathered = jnp.where(
        lax.broadcasted_iota(jnp.int32, (half, boxes), 0) == box_of // fold, 1.0, 0.0
    ).astype(BF16)

    def far_part(n):
        copy_of(bit_count, n).wait_recv()
        own = mine[n].astype(F32)
        other = theirs[n].astype(F32)
        for s, piece in enumerate((jnp.where(src_first, own, other), jnp.where(src_first, other, own))):
            for h in range(per):
                coeff[n, pl.ds(s * per + h, 2 * rank, stride=group), :] = piece[:, h * boxes:(h + 1) * boxes]
        many = 8

        def far_step(g, carry):
            rows = pl.ds(pl.multiple_of(g * many, many), many)
            flat = pl.ds(pl.multiple_of(g * many * group, many * group), many * group)
            real_acc = near[n, 0, flat, :].reshape(many, group, boxes)
            imag_acc = near[n, 1, flat, :].reshape(many, group, boxes)
            for r in range(rank):
                real = coeff[n, r * group:(r + 1) * group, :][None]
                imag = coeff[n, (rank + r) * group:(rank + r + 1) * group, :][None]
                w_real = basis[0, rows, r:r + 1, :]
                w_imag = basis[1, rows, r:r + 1, :]
                real_acc = real_acc + w_real * real - w_imag * imag
                imag_acc = imag_acc + w_real * imag + w_imag * real
            near[n, 0, flat, :] = real_acc.reshape(many * group, boxes)
            near[n, 1, flat, :] = imag_acc.reshape(many * group, boxes)
            return carry

        lax.fori_loop(0, half // many, far_step, 0)

    def turn_part(n):
        for c in range(2):
            for s in range(sources):
                for h in range(per):
                    plane = near[n, c, pl.ds(s * per + h, half, stride=group), :]
                    masked = [jnp.where(box_of % fold == k, plane, 0.0).astype(BF16) for k in range(fold)]
                    moved = lax.dot_general(
                        gathered, jnp.concatenate(masked, axis=0), (((1,), (1,)), ((), ())),
                        preferred_element_type=F32,
                    )
                    at = (s * width + n * per + h) * half
                    turned[c, at:at + half, :] = moved

    slots = [4, 2, 2, 1, 1]
    for at, (bit, n) in enumerate(plan(bit_count)):
        last = bit == bit_count - 1
        if last and n == 0:
            loads[6].wait()
            basis[...] = basis_ref[...].astype(F32)
        elif at < len(slots):
            near_part(slots[at])
        copy_of(bit, n).wait_recv()
        upper = (lax.axis_index("tgt") // 2**bit) % 2
        own = vals[n]
        other = came[bit, n].astype(F32)
        is_upper = jnp.broadcast_to(upper, own.shape) == 1
        stacked = join(jnp.where(is_upper, other, own), jnp.where(is_upper, own, other))
        s_high, s_low = split(stacked)
        mixed = dot(cross_high[bit], s_high) + dot(cross_high[bit], s_low) + dot(cross_low[bit], s_high)
        if last:
            mine[n] = mixed.astype(BF16)
        else:
            vals[n] = mixed
            sent[bit + 1, n] = mixed.astype(BF16)
        copy_of(bit + 1, n).start()
        if last:
            if n < CHUNKS - 1:
                near_part(near_total if n == CHUNKS - 2 else 2)
            else:
                for earlier in range(n):
                    turn_part(earlier)
            far_part(n)
    turn_part(CHUNKS - 1)
    lanes = fold * half
    for c in range(2):
        for t in range(half):
            out_ref[c, :, t * lanes:(t + 1) * lanes] = turned[c, pl.ds(t, rhs, stride=half), :].astype(BF16)
    for k in range(pieces):
        half_copy(k).wait_send()
    for bit in range(bit_count + 1):
        for n in range(CHUNKS):
            copy_of(bit, n).wait_send()


def on_device(sources, leaf_order, skeleton, interp_rows, near_tiles, target_basis, level_maps):
    tgt_count = lax.axis_size("tgt")
    src_count = lax.axis_size("src")
    point_count, rhs = sources.shape
    boxes, rank = skeleton.shape
    leaf = interp_rows.shape[3]
    half = leaf // src_count
    width = rhs // src_count
    size = width * boxes // CHUNKS
    group = rhs // CHUNKS
    local_levels = boxes.bit_length() - 1
    bits = tgt_count.bit_length() - 1
    operands = (
        sources.T, leaf_order.reshape(point_count // boxes, boxes), skeleton.T,
        interp_rows.transpose(0, 2, 3, 1), near_tiles.transpose(0, 2, 3, 1),
        target_basis.transpose(0, 2, 3, 1), level_maps,
    )
    vmem = pltpu.VMEM
    dma = pltpu.SemaphoreType.DMA
    field = pl.pallas_call(
        lambda *refs: kernel(local_levels, bits, *refs),
        out_shape=jax.ShapeDtypeStruct((2, rhs, point_count), BF16),
        in_specs=[pl.BlockSpec(memory_space=pl.ANY)] * len(operands),
        out_specs=pl.BlockSpec(memory_space=pltpu.VMEM),
        scratch_shapes=[vmem(operand.shape, operand.dtype) for operand in operands] + [
            vmem((point_count // LOW * rhs, LOW), BF16),
            vmem((half, boxes), jnp.int32),
            vmem((half, boxes), jnp.int32),
            vmem((half, rhs, boxes), BF16),
            vmem((half, rhs, boxes), BF16),
            vmem((leaf, width, boxes), F32),
            vmem((8, leaf, boxes), F32),
            vmem((2 * rank * width, boxes), F32),
            vmem((local_levels, 4 * rank, 8 * rank), BF16),
            vmem((local_levels, 4 * rank, 4 * rank), BF16),
            vmem((bits, 2 * rank, 4 * rank), BF16),
            vmem((bits, 2 * rank, 4 * rank), BF16),
            vmem((CHUNKS, 2 * rank, size), F32),
            vmem((bits, CHUNKS, 2 * rank, size), BF16),
            vmem((bits, CHUNKS, 2 * rank, size), BF16),
            vmem((CHUNKS, 2 * rank, size), BF16),
            vmem((CHUNKS, 2 * rank, size), BF16),
            vmem((leaf, rhs, boxes), F32),
            vmem((CHUNKS, 2, half * group, boxes), F32),
            vmem((2, half, rank, boxes), F32),
            vmem((CHUNKS, 2 * rank * group, boxes), F32),
            vmem((2, rhs * half, boxes), F32),
            dma((len(operands),)),
            dma((bits + 1, CHUNKS)),
            dma((bits + 1, CHUNKS)),
            dma((2,)),
            dma((2,)),
        ],
        compiler_params=pltpu.CompilerParams(
            vmem_limit_bytes=60 * 2**20, collective_id=0, has_side_effects=True
        ),
    )(*operands)
    return field.transpose(0, 2, 1)


def solution(mesh):
    return jax.shard_map(
        on_device,
        mesh=mesh,
        in_specs=(
            P(("grp", "tgt", "src"), None),
            P(("grp", "tgt", "src")),
            P(("grp", "tgt"), None),
            P(None, ("grp", "tgt"), None, None),
            P(None, ("grp", "tgt"), "src", None),
            P(None, ("grp", "tgt"), "src", None),
            P(None, "grp", None, None, None),
        ),
        out_specs=P(None, ("grp", "tgt", "src"), None),
        check_vma=False,
    )
```
